32 devices in a mesh: dp: 8 (over y, x, core), owner: 4 (over z).
Axes of the slice: x: 2, y: 2, z: 4, core: 2. Of those that a mesh axis runs over, the one named last changes fastest.
Arguments:
- line_columns: bfloat16 [4, 16384, 512], P(None, ('dp', 'owner')), may hold values from -12 to 12
- line_widths: int32 [32, 4], P(('dp', 'owner')), may hold values from 1 to 128, as said below
- layer_owner: int32 [4], replicated, may hold values from 0 to 3, each once
Outputs:
- preconditioned: float32 [4, 1152, 128], replicated
The draws below stay inside these ranges and needn't reach their ends.
Inputs may be any that keep to these rules, and one draw needn't show every extreme that they name: `line_widths`: row b holds the widths of the 4 lines of device b, laid end to end from its first position; in every draw the lines of some device all have width 128.
All inputs are finite; a program needn't handle non-finite values.
Results may differ from the reference program's by a relative error of at most 0.0003.
Values may be sent and summed in bfloat16 or wider, within the bound.
A program may use at most 128 MiB of HBM per device.

```python
import math
import jax
import jax.numpy as jnp
from jax import lax

C = 128
WMAX = 128
LINES_DEV = 4
POS_DEV = 512
ROWS = 16384
LAYERS = 4
DEVICES = 32


filter_ratio = 0.88


filter_taps = 16


def filter_norm():
    total = 0.0
    for tap in range(filter_taps):
        total = total + filter_ratio ** (2 * tap)
    return 1.0 / math.sqrt(total)


def draw_line_columns(key, part):
    layer_key = jax.random.fold_in(key, 11)
    channel_norm = filter_norm()

    def one_layer(layer_index):
        keys = jax.random.split(jax.random.fold_in(layer_key, layer_index), 12)
        source = jax.random.normal(keys[0], (ROWS + 1, 3 * C), jnp.float32)
        row_spread = 0.6
        temporal = source[1:] + 0.6 * source[:-1]
        features = jnp.zeros_like(temporal)
        for tap in range(filter_taps):
            features = features + filter_ratio ** tap * jnp.roll(temporal, tap, axis=1)
        features = features * channel_norm
        column_scale = jnp.exp(jax.random.uniform(keys[1], (1, 3 * C), jnp.float32, -0.8, 0.8))
        row_noise = jax.random.uniform(keys[2], (DEVICES, POS_DEV, 1), jnp.float32, -row_spread, row_spread)
        device_noise = jax.random.uniform(keys[3], (DEVICES, 1, 1), jnp.float32, -0.45, 0.45)
        rising = 0.55 * jnp.arange(DEVICES, dtype=jnp.float32)[:, None, None] / max(DEVICES - 1, 1) - 0.3
        row_scale = jnp.exp(row_noise + device_noise + rising).reshape(ROWS, 1)
        features = features * column_scale * row_scale
        mixing = jax.random.uniform(keys[4], (DEVICES, 1, 1), jnp.float32, -1.5, 1.5)
        mixing = jnp.broadcast_to(mixing, (DEVICES, POS_DEV, 1)).reshape(ROWS, 1)
        gradients = 0.7 * jax.random.normal(keys[5], (ROWS, C), jnp.float32) * row_scale
        for tap_index, shift_size in ((0, 0), (1, 5), (2, 11)):
            base_coef = jax.random.uniform(keys[6 + tap_index], (1, C), jnp.float32, -0.8, 0.8)
            varying = jax.random.uniform(keys[9 + tap_index], (1, C), jnp.float32, -0.8, 0.8)
            channel_part = features[:, tap_index * C:(tap_index + 1) * C]
            gradients = gradients + (base_coef + mixing * varying) * jnp.roll(channel_part, shift_size, axis=1)
        values = jnp.concatenate([features, gradients], axis=1)
        return jnp.clip(values, -12.0, 12.0).astype(jnp.bfloat16)
    return lax.map(one_layer, jnp.arange(LAYERS, dtype=jnp.int32))


def draw_line_widths(key, part):
    keys = jax.random.split(jax.random.fold_in(key, 23), 3)
    bucket_top = jax.random.randint(keys[0], (), WMAX // 4, WMAX + 1, jnp.int32)
    raw_widths = jax.random.randint(keys[1], (DEVICES, LINES_DEV), 0, WMAX, jnp.int32)
    widths = 1 + raw_widths % bucket_top
    full_row = jax.random.randint(keys[2], (), 0, DEVICES, jnp.int32)
    device_rows = jnp.arange(DEVICES, dtype=jnp.int32)[:, None]
    return jnp.where(device_rows == full_row, WMAX, widths).astype(jnp.int32)


def setup_inputs(seed: int = 0) -> dict:
    key_list = jax.random.split(jax.random.key(seed), 4)
    line_columns = draw_line_columns(jax.random.fold_in(key_list[3], 71), 0)
    line_widths = draw_line_widths(jax.random.fold_in(key_list[3], 71), 0)
    layer_owner = jax.random.permutation(key_list[2], LAYERS).astype(jnp.int32)
    return {"line_columns": line_columns, "line_widths": line_widths, "layer_owner": layer_owner}


damping = 0.1

def patch_columns(block, widths):
    positions = block.shape[-2]
    channels = block.shape[-1] // 4
    line_ends = jnp.cumsum(widths, axis=-1).astype(jnp.int32)
    line_starts = line_ends - widths
    place = jnp.arange(positions, dtype=jnp.int32)[:, None]
    opening = jnp.any(place == line_starts[..., None, :], axis=-1)[..., None]
    closing = jnp.any(place + 1 == line_ends[..., None, :], axis=-1)[..., None]
    inside = place < line_ends[..., None, -1:]
    features = block[..., :3 * channels]
    gradients = block[..., 3 * channels:]
    padding = jnp.zeros_like(features[..., :1, :])
    before = jnp.concatenate([padding, features[..., :-1, :]], axis=-2)
    after = jnp.concatenate([features[..., 1:, :], padding], axis=-2)
    before = jnp.where(opening, jnp.zeros_like(before), before)
    after = jnp.where(closing, jnp.zeros_like(after), after)
    stacked = jnp.concatenate([before, features, after, gradients], axis=-1)
    return jnp.where(inside, stacked, jnp.zeros_like(stacked))

def precondition(factor, total_rows):
    full_width = factor.shape[0]
    patch_width = full_width // 10 * 9
    scaled = factor / total_rows
    act_factor = scaled[:patch_width, :patch_width] + damping * jnp.eye(patch_width, dtype=factor.dtype)
    grad_factor = scaled[patch_width:, patch_width:] + damping * jnp.eye(full_width - patch_width, dtype=factor.dtype)
    cross_term = scaled[:patch_width, patch_width:]
    act_cholesky = jnp.linalg.cholesky(act_factor)
    left_solved = jax.scipy.linalg.cho_solve((act_cholesky, True), cross_term)
    grad_cholesky = jnp.linalg.cholesky(grad_factor)
    return jax.scipy.linalg.cho_solve((grad_cholesky, True), left_solved.T).T

def reference(line_columns, line_widths, layer_owner):
    results = []
    for slot in range(LAYERS):
        layer_block = lax.dynamic_index_in_dim(line_columns, layer_owner[slot], 0, keepdims=False)
        layer_block = layer_block.reshape(DEVICES, POS_DEV, 4 * C)

        def add_block(running, pieces):
            columns = patch_columns(pieces[0], pieces[1])
            return (running + jnp.dot(columns.T.astype(jnp.float32), columns.astype(jnp.float32), preferred_element_type=jnp.float32), None)
        factor, _ = lax.scan(add_block, jnp.zeros((10 * C, 10 * C), jnp.float32), (layer_block, line_widths))
        results.append(precondition(factor, ROWS))
    return jnp.stack(results)
```

```python
import functools

import jax
import jax.numpy as jnp
from jax import lax
from jax.experimental import pallas as pl
from jax.experimental.pallas import tpu as pltpu
from jax.sharding import PartitionSpec as P

damping = 0.1
tile = 128
HIGHEST = lax.Precision.HIGHEST


def invert_tile(matrix):
    groups = tile // 8
    rows = [matrix[8 * i:8 * i + 8, :] for i in range(groups)]
    lane = lax.broadcasted_iota(jnp.int32, (8, tile), 1)
    sub = lax.broadcasted_iota(jnp.int32, (8, tile), 0)
    for p in range(groups):
        low = 8 * p
        in_panel = (lane >= low) & (lane < low + 8)
        unit = jnp.where(lane - low == sub, 1.0, 0.0)
        panel = jnp.where(in_panel, unit, rows[p])
        pivot = [jnp.broadcast_to(rows[p][:, low + j:low + j + 1], (8, tile)) for j in range(8)]
        for j in range(8):
            inverse = 1.0 / pivot[j][j:j + 1, :]
            for m in range(j + 1, 8):
                scaled = pivot[m][j:j + 1, :] * inverse
                pivot[m] = jnp.where(sub == j, scaled, pivot[m] - pivot[j] * scaled)
            scaled = panel[j:j + 1, :] * inverse
            panel = jnp.where(sub == j, scaled, panel - pivot[j] * scaled)
        for i in range(groups):
            if i == p:
                continue
            total = jnp.where(in_panel, 0.0, rows[i])
            for j in range(8):
                column = jnp.broadcast_to(rows[i][:, low + j:low + j + 1], (8, tile))
                total = total - column * panel[j:j + 1, :]
            rows[i] = total
        rows[p] = panel
    return jnp.concatenate(rows, axis=0)


def dot(a, b):
    return jnp.dot(a, b, precision=HIGHEST, preferred_element_type=jnp.float32)


def solve_kernel(scale, gram_ref, out_ref, work, solved):
    packed = gram_ref.shape[0]
    ch = packed // 4
    feat = 3 * ch
    n = 3 * feat
    blocks = n // tile
    first, second, third = packed, 2 * packed, 2 * packed + feat
    fourth = third + feat

    def gram(rows, cols):
        return gram_ref[rows, cols] * scale

    xs = slice(0, feat)
    eye = jnp.where(
        lax.broadcasted_iota(jnp.int32, (feat, feat), 0)
        == lax.broadcasted_iota(jnp.int32, (feat, feat), 1), damping, 0.0)
    centre = gram(xs, slice(0, feat)) + eye
    ahead = gram(xs, slice(first, first + feat))
    work[...] = jnp.zeros_like(work)
    work[0:feat, 0:feat] = centre - gram(xs, slice(third, fourth))
    work[0:feat, feat:2 * feat] = ahead
    work[0:feat, 2 * feat:n] = gram(xs, slice(second, third))
    work[feat:2 * feat, feat:2 * feat] = centre
    work[feat:2 * feat, 2 * feat:n] = ahead
    work[2 * feat:n, 2 * feat:n] = centre - gram(xs, slice(fourth, fourth + feat))
    work[0:feat, n:n + ch] = gram(xs, slice(first + feat, first + packed))
    work[feat:2 * feat, n:n + ch] = gram(xs, slice(feat, packed))
    work[2 * feat:n, n:n + ch] = gram(slice(feat, packed), slice(first, first + feat)).T
    work[n:n + ch, 0:ch] = gram(slice(feat, packed), slice(feat, packed)) + eye[:ch, :ch]

    def eliminate(j, carry):
        top = pl.ds(pl.multiple_of(j * tile, tile), tile)
        col = pl.multiple_of(jnp.where(j == blocks, 0, j) * tile, tile)
        inverse = invert_tile(work[top, pl.ds(col, tile)])

        @pl.when(j < blocks)
        def _():
            row = dot(inverse, work[top, :])
            solved[top, :] = row

            def update(i, carry):
                where = pl.ds(pl.multiple_of(i * tile, tile), tile)
                work[where, :] -= dot(work[top, where].T, solved[top, :])
                return carry

            lax.fori_loop(j + 1, blocks, update, 0)

        @pl.when(j == blocks)
        def _():
            solved[top, 0:tile] = inverse

        return carry

    lax.fori_loop(0, blocks + 1, eliminate, 0)

    out_ref[...] = jnp.zeros_like(out_ref)

    def back(step, carry):
        j = blocks - 1 - step
        top = pl.ds(pl.multiple_of(j * tile, tile), tile)
        out_ref[top, :] = solved[top, n:n + ch] - dot(solved[top, 0:n], out_ref[...])
        return carry

    lax.fori_loop(0, blocks, back, 0)
    out_ref[...] = dot(out_ref[...], solved[n:n + ch, 0:ch])


def precondition(gram, total_rows):
    packed = gram.shape[0]
    ch = packed // 4
    n = 9 * ch
    return pl.pallas_call(
        functools.partial(solve_kernel, 1.0 / total_rows),
        out_shape=jax.ShapeDtypeStruct((n, ch), jnp.float32),
        in_specs=[pl.BlockSpec(memory_space=pltpu.VMEM)],
        out_specs=pl.BlockSpec(memory_space=pltpu.VMEM),
        scratch_shapes=[
            pltpu.VMEM((n + ch, n + ch), jnp.float32),
            pltpu.VMEM((n + ch, n + ch), jnp.float32),
        ],
        compiler_params=pltpu.CompilerParams(vmem_limit_bytes=48 * 2 ** 20),
    )(gram)


def line_masks(widths, positions):
    ends = jnp.cumsum(widths, axis=-1).astype(jnp.int32)
    starts = ends - widths
    place = jnp.arange(positions, dtype=jnp.int32)[:, None]
    inside = place < ends[..., None, -1:]
    opening = jnp.any(place == starts[..., None, :], axis=-1, keepdims=True)
    closing = jnp.any(place + 1 == ends[..., None, :], axis=-1, keepdims=True)
    return inside, opening, closing


def shifted(block):
    return jnp.concatenate([block[..., 1:, :], jnp.zeros_like(block[..., :1, :])], axis=-2)


def body(line_columns, line_widths, layer_owner):
    layer_count, positions, packed = line_columns.shape
    ch = packed // 4
    feat = 3 * ch
    n_replicas = lax.axis_size("dp")
    n_owners = lax.axis_size("owner")
    total_rows = n_replicas * n_owners * positions
    ordered = jnp.take(line_columns, layer_owner, axis=0)
    width_copies = jnp.broadcast_to(line_widths[None, :, :], (n_owners, 1, line_widths.shape[1]))
    received = lax.all_to_all(ordered, "owner", split_axis=0, concat_axis=1, tiled=True)
    source_widths = lax.all_to_all(width_copies, "owner", split_axis=0, concat_axis=1, tiled=True)
    blocks = received.reshape(n_owners, positions, packed)
    inside, opening, closing = line_masks(source_widths.reshape(n_owners, -1), positions)
    zero = jnp.zeros((), blocks.dtype)
    live = jnp.where(inside, blocks, zero)
    ahead = jnp.where(closing, zero, shifted(live))
    ahead2 = jnp.where(closing, zero, shifted(ahead[..., :feat]))
    last = jnp.where(closing, live[..., :feat], zero)
    start = jnp.where(opening & inside, live[..., :feat], zero)
    right = jnp.concatenate([live, ahead, ahead2, last, start], axis=-1)
    gram = lax.dot_general(
        live.reshape(-1, packed), right.reshape(n_owners * positions, -1),
        (((0,), (0,)), ((), ())), preferred_element_type=jnp.float32)
    gram = lax.psum(gram, "dp")
    result = precondition(gram, total_rows)
    return lax.all_gather(result[None], "owner", axis=0, tiled=True)


def solution(mesh):
    in_specs = (P(None, ("dp", "owner"), None), P(("dp", "owner"), None), P())
    return jax.shard_map(body, mesh=mesh, in_specs=in_specs, out_specs=P(), check_vma=False)
```

```python
import functools

import jax
import jax.numpy as jnp
from jax import lax
from jax.experimental import pallas as pl
from jax.experimental.pallas import tpu as pltpu
from jax.sharding import PartitionSpec as P

damping = 0.1
tile = 128
HIGHEST = lax.Precision.HIGHEST


def invert_tile(matrix):
    groups = tile // 8
    rows = [matrix[8 * i:8 * i + 8, :] for i in range(groups)]
    lane = lax.broadcasted_iota(jnp.int32, (8, tile), 1)
    sub = lax.broadcasted_iota(jnp.int32, (8, tile), 0)
    for p in range(groups):
        low = 8 * p
        in_panel = (lane >= low) & (lane < low + 8)
        unit = jnp.where(lane - low == sub, 1.0, 0.0)
        panel = jnp.where(in_panel, unit, rows[p])
        pivot = [jnp.broadcast_to(rows[p][:, low + j:low + j + 1], (8, tile)) for j in range(8)]
        for j in range(8):
            inverse = 1.0 / pivot[j][j:j + 1, :]
            for m in range(j + 1, 8):
                scaled = pivot[m][j:j + 1, :] * inverse
                pivot[m] = jnp.where(sub == j, scaled, pivot[m] - pivot[j] * scaled)
            scaled = panel[j:j + 1, :] * inverse
            panel = jnp.where(sub == j, scaled, panel - pivot[j] * scaled)
        for i in range(groups):
            if i == p:
                continue
            total = jnp.where(in_panel, 0.0, rows[i])
            for j in range(8):
                column = jnp.broadcast_to(rows[i][:, low + j:low + j + 1], (8, tile))
                total = total - column * panel[j:j + 1, :]
            rows[i] = total
        rows[p] = panel
    return jnp.concatenate(rows, axis=0)


def dot(a, b):
    return jnp.dot(a, b, precision=HIGHEST, preferred_element_type=jnp.float32)


upper = [(r, c) for r in range(3) for c in range(r, 3)]
square = [(r, c) for r in range(3) for c in range(3)]
tiles = (
    upper + [(r, 3) for r in range(3)] + [(3, 3)]
    + [(r, c + 4) for r, c in square] + [(r, 7) for r in range(3)] + [(3, c + 4) for c in range(3)]
    + [(r, c + 8) for r, c in square]
    + [(r, c + 11) for r, c in upper] + [(r, c + 14) for r, c in upper]
)
halves, quarters, share = 2, 4, 6
place_of = {t: (i // (quarters * share), i // share % quarters, i % share) for i, t in enumerate(tiles)}


def solve_kernel(scale, gram_ref, out_ref, work, solved):
    ch = tile
    n = 9 * ch
    blocks = 9
    eye = jnp.where(
        lax.broadcasted_iota(jnp.int32, (ch, ch), 0)
        == lax.broadcasted_iota(jnp.int32, (ch, ch), 1), damping, 0.0)

    def gram(r, c):
        h, q, s = place_of[(r, c)]
        return gram_ref[h, q, s] * scale

    def put(r, c, value):
        work[r * ch:(r + 1) * ch, c * ch:(c + 1) * ch] = value

    work[...] = jnp.zeros_like(work)
    for r in range(3):
        for c in range(r, 3):
            centre = gram(r, c) + eye if r == c else gram(r, c)
            put(r, c, centre - gram(r, c + 11))
            put(r + 3, c + 3, centre)
            put(r + 6, c + 6, centre - gram(r, c + 14))
        for c in range(3):
            ahead = gram(r, c + 4)
            put(r, c + 3, ahead)
            put(r + 3, c + 6, ahead)
            put(r, c + 6, gram(r, c + 8))
        put(r, 9, gram(r, 7))
        put(r + 3, 9, gram(r, 3))
        put(r + 6, 9, gram(3, r + 4).T)
    put(9, 0, gram(3, 3) + eye)

    def eliminate(j, carry):
        top = pl.ds(pl.multiple_of(j * tile, tile), tile)
        col = pl.multiple_of(jnp.where(j == blocks, 0, j) * tile, tile)
        inverse = invert_tile(work[top, pl.ds(col, tile)])

        @pl.when(j < blocks)
        def _():
            row = dot(inverse, work[top, :])
            solved[top, :] = row

            def update(i, carry):
                where = pl.ds(pl.multiple_of(i * tile, tile), tile)
                work[where, :] -= dot(work[top, where].T, solved[top, :])
                return carry

            lax.fori_loop(j + 1, blocks, update, 0)

        @pl.when(j == blocks)
        def _():
            solved[top, 0:tile] = inverse

        return carry

    lax.fori_loop(0, blocks + 1, eliminate, 0)

    out_ref[...] = jnp.zeros_like(out_ref)

    def back(step, carry):
        j = blocks - 1 - step
        top = pl.ds(pl.multiple_of(j * tile, tile), tile)
        out_ref[top, :] = solved[top, n:n + ch] - dot(solved[top, 0:n], out_ref[...])
        return carry

    lax.fori_loop(0, blocks, back, 0)
    out_ref[...] = dot(out_ref[...], solved[n:n + ch, 0:ch])


def precondition(gram, total_rows):
    n = 9 * tile
    return pl.pallas_call(
        functools.partial(solve_kernel, 1.0 / total_rows),
        out_shape=jax.ShapeDtypeStruct((n, tile), jnp.float32),
        in_specs=[pl.BlockSpec(memory_space=pltpu.VMEM)],
        out_specs=pl.BlockSpec(memory_space=pltpu.VMEM),
        scratch_shapes=[
            pltpu.VMEM((n + tile, n + tile), jnp.float32),
            pltpu.VMEM((n + tile, n + tile), jnp.float32),
        ],
        compiler_params=pltpu.CompilerParams(vmem_limit_bytes=48 * 2 ** 20),
    )(gram)


def pack_tiles(gram):
    parts = [gram[r * tile:(r + 1) * tile, c * tile:(c + 1) * tile] for r, c in tiles]
    parts += [jnp.zeros((tile, tile), gram.dtype)] * (halves * quarters * share - len(tiles))
    return jnp.stack(parts).reshape(halves, quarters, share, tile, tile)


def line_masks(widths, positions):
    ends = jnp.cumsum(widths, axis=-1).astype(jnp.int32)
    starts = ends - widths
    place = jnp.arange(positions, dtype=jnp.int32)[:, None]
    inside = place < ends[..., None, -1:]
    opening = jnp.any(place == starts[..., None, :], axis=-1, keepdims=True)
    closing = jnp.any(place + 1 == ends[..., None, :], axis=-1, keepdims=True)
    return inside, opening, closing


def shifted(block):
    return jnp.concatenate([block[..., 1:, :], jnp.zeros_like(block[..., :1, :])], axis=-2)


def body(line_columns, line_widths, layer_owner):
    layer_count, positions, packed = line_columns.shape
    ch = packed // 4
    feat = 3 * ch
    n_replicas = lax.axis_size("dp")
    n_owners = lax.axis_size("owner")
    total_rows = n_replicas * n_owners * positions
    ordered = jnp.take(line_columns, layer_owner, axis=0)
    width_copies = jnp.broadcast_to(line_widths[None, :, :], (n_owners, 1, line_widths.shape[1]))
    received = lax.all_to_all(ordered, "owner", split_axis=0, concat_axis=1, tiled=True)
    source_widths = lax.all_to_all(width_copies, "owner", split_axis=0, concat_axis=1, tiled=True)
    blocks = received.reshape(n_owners, positions, packed)
    inside, opening, closing = line_masks(source_widths.reshape(n_owners, -1), positions)
    zero = jnp.zeros((), blocks.dtype)
    live = jnp.where(inside, blocks, zero)
    ahead = jnp.where(closing, zero, shifted(live))
    ahead2 = jnp.where(closing, zero, shifted(ahead[..., :feat]))
    last = jnp.where(closing, live[..., :feat], zero)
    start = jnp.where(opening & inside, live[..., :feat], zero)
    right = jnp.concatenate([live, ahead, ahead2, last, start], axis=-1)
    gram = lax.dot_general(
        live.reshape(-1, packed), right.reshape(n_owners * positions, -1),
        (((0,), (0,)), ((), ())), preferred_element_type=jnp.float32)
    gram = lax.psum(pack_tiles(gram), "dp")
    result = precondition(gram, total_rows)
    return lax.all_gather(result[None], "owner", axis=0, tiled=True)


def device(column, core, z):
    return {"dp": 2 * column + core, "owner": z}


def send(src, dst, sems, slot, to):
    return pltpu.make_async_remote_copy(
        src_ref=src, dst_ref=dst, send_sem=sems.at[0, slot], recv_sem=sems.at[1, slot],
        device_id=to, device_id_type=pl.DeviceIdType.MESH)


def here():
    index = lax.axis_index("dp")
    return index // 2, index % 2, lax.axis_index("owner")


def greet(partners):
    barrier = pltpu.get_barrier_semaphore()
    for partner in partners:
        pl.semaphore_signal(barrier, inc=1, device_id=partner, device_id_type=pl.DeviceIdType.MESH)
    return barrier


def block_products(rows_ref, info_ref, gram, first):
    positions, packed = rows_ref.shape
    feat = packed // 4 * 3
    place = lax.broadcasted_iota(jnp.int32, (positions, tile), 0)
    info = info_ref[...]
    lines = info.shape[0] // 2

    def any_of(rows, at):
        hit = at == info[rows[0]:rows[0] + 1, :]
        for r in rows[1:]:
            hit = hit | (at == info[r:r + 1, :])
        return hit

    inside = place < info[2 * lines - 1:2 * lines, :]
    opening = any_of(range(lines), place) & inside
    closing = any_of(range(lines, 2 * lines), place + 1)

    def mask(flag, width):
        return jnp.tile(jnp.where(flag, 1.0, 0.0), (1, width // tile))

    def up(value):
        return pltpu.roll(value, positions - 1, 0)

    inner = mask(inside & ~closing, packed)
    live = rows_ref[...].astype(jnp.float32) * mask(inside, packed)
    ahead = up(live) * inner
    ahead2 = up(ahead[:, :feat]) * inner[:, :feat]
    last = live[:, :feat] * mask(closing, feat)
    start = live[:, :feat] * mask(opening, feat)
    left = live.astype(jnp.bfloat16).T
    at = 0
    for part in (live, ahead, ahead2, last, start):
        cols = slice(at, at + part.shape[1])
        product = jnp.dot(left, part.astype(jnp.bfloat16), preferred_element_type=jnp.float32)
        if first:
            gram[:, cols] = product
        else:
            gram[:, cols] += product
        at += part.shape[1]


def reduce_kernel(rows_ref, info_ref, full, rows_in, info_in, gram, part, core_in, acc,
                  right_out, left_out, right_in, left_in,
                  row_sems, info_sems, core_sems, right_sems, left_sems,
                  ahead_sems, behind_sems, share_sems):
    column, core, z = here()
    top = quarters - 1
    peers = [device(column ^ k, core, z) for k in (1, 2, 3)]
    sibling = device(column, 1 - core, z)
    right, left = device(column, core, z + 1), device(column, core, z - 1)
    barrier = greet(peers + [sibling])

    @pl.when(z < top)
    def _():
        pl.semaphore_signal(barrier, inc=1, device_id=right, device_id_type=pl.DeviceIdType.MESH)

    @pl.when(z > 0)
    def _():
        pl.semaphore_signal(barrier, inc=1, device_id=left, device_id_type=pl.DeviceIdType.MESH)

    pl.semaphore_wait(barrier, 4 + jnp.where(z < top, 1, 0) + jnp.where(z > 0, 1, 0))

    rows_out = []
    for k in (1, 2, 3):
        note = send(info_ref, info_in.at[k - 1], info_sems, k - 1, peers[k - 1])
        note.start()
        copy = send(rows_ref.at[column ^ k], rows_in.at[k - 1], row_sems, k - 1, peers[k - 1])
        copy.start()
        rows_out.append((note, copy))
    block_products(rows_ref.at[column], info_ref, gram, True)
    for k in (1, 2, 3):
        for copy in rows_out[k - 1]:
            copy.wait_recv()
        block_products(rows_in.at[k - 1], info_in.at[k - 1], gram, False)

    for t, (h, q, s) in place_of.items():
        r, c = t
        part[h, q, s] = gram[r * tile:(r + 1) * tile, c * tile:(c + 1) * tile]
    for i in range(len(tiles), halves * quarters * share):
        part[i // (quarters * share), i // share % quarters, i % share] = jnp.zeros((tile, tile), jnp.float32)

    order = (3, 0, 2, 1)
    core_out = {}
    for q in order:
        core_out[q] = send(part.at[1 - core, q], core_in.at[q], core_sems, q, sibling)
        core_out[q].start()
    for q in order:
        core_out[q].wait_recv()
        acc[q] = part[core, q] + core_in[q]

    def hop(q, out, into, sems, to):
        return send(out.at[q], into.at[q], sems, q, to)

    for step in range(top):
        for q, out, into, sems, to, sends, first in (
            (top - step, right_out, right_in, right_sems, right, z < top - step, z == 0),
            (step, left_out, left_in, left_sems, left, z > step, z == top),
        ):
            takes = (z > 0) & (z <= q) if out is right_out else (z < top) & (z >= q)
            copy = hop(q, out, into, sems, to)

            @pl.when(takes)
            def _(copy=copy):
                copy.wait_recv()

            @pl.when(sends & first)
            def _(copy=copy, q=q, out=out):
                out[q] = acc[q]
                copy.start()

            @pl.when(sends & ~first)
            def _(copy=copy, q=q, out=out, into=into):
                out[q] = acc[q] + into[q]
                copy.start()

    full[core, z] = acc[z]

    @pl.when(z > 0)
    def _():
        full[core, z] += right_in[z]

    @pl.when(z < top)
    def _():
        full[core, z] += left_in[z]

    def give(q, sems, to):
        return send(full.at[core, q], full.at[core, q], sems, q, to)

    def share_with_sibling(q):
        return send(full.at[core, q], full.at[core, q], share_sems, q, sibling)

    share_with_sibling(z).start()
    for step in range(top):
        @pl.when((z < top) & (z - step >= 0))
        def _(step=step):
            give(z - step, ahead_sems, right).start()

        @pl.when((z > 0) & (z + step <= top))
        def _(step=step):
            give(z + step, behind_sems, left).start()

        @pl.when(z - step - 1 >= 0)
        def _(step=step):
            q = z - step - 1
            give(q, ahead_sems, left).wait_recv()
            share_with_sibling(q).start()

        @pl.when(z + step + 1 <= top)
        def _(step=step):
            q = z + step + 1
            give(q, behind_sems, right).wait_recv()
            share_with_sibling(q).start()

    for q in range(quarters):
        send(full.at[1 - core, q], full.at[1 - core, q], share_sems, q, sibling).wait_recv()

    for pair in rows_out:
        for copy in pair:
            copy.wait_send()
    for q in range(quarters):
        core_out[q].wait_send()
        share_with_sibling(q).wait_send()

        @pl.when(z < q)
        def _(q=q):
            hop(q, right_out, right_in, right_sems, right).wait_send()

        @pl.when(z > q)
        def _(q=q):
            hop(q, left_out, left_in, left_sems, left).wait_send()

        @pl.when((z < top) & (z >= q))
        def _(q=q):
            give(q, ahead_sems, right).wait_send()

        @pl.when((z > 0) & (z <= q))
        def _(q=q):
            give(q, behind_sems, left).wait_send()


def reduced_gram(rows, info):
    columns, positions, packed = rows.shape
    wide = 4 * packed + tile
    quarter = (quarters, share, tile, tile)
    vmem = pl.BlockSpec(memory_space=pltpu.VMEM)
    return pl.pallas_call(
        reduce_kernel,
        out_shape=jax.ShapeDtypeStruct((halves,) + quarter, jnp.float32),
        in_specs=[vmem, vmem],
        out_specs=vmem,
        scratch_shapes=[
            pltpu.VMEM((3, positions, packed), rows.dtype),
            pltpu.VMEM((3,) + info.shape, info.dtype),
            pltpu.VMEM((packed, wide), jnp.float32),
            pltpu.VMEM((halves,) + quarter, jnp.float32),
        ] + [pltpu.VMEM(quarter, jnp.float32)] * 6 + [
            pltpu.SemaphoreType.DMA((2, 3)),
            pltpu.SemaphoreType.DMA((2, 3)),
        ] + [pltpu.SemaphoreType.DMA((2, quarters))] * 6,
        compiler_params=pltpu.CompilerParams(
            collective_id=0, has_side_effects=True, vmem_limit_bytes=48 * 2 ** 20),
    )(rows, info)


def spread_kernel(result_ref, out_ref, sems, share_sems):
    column, core, z = here()
    n = result_ref.shape[0]
    rows = n // 2
    peers = [device(column ^ k, core, z) for k in (1, 2, 3)]
    sibling = device(column, 1 - core, z)
    pl.semaphore_wait(greet(peers + [sibling]), 4)
    mine = pl.ds(pl.multiple_of(core * rows, 8), rows)
    other = pl.ds(pl.multiple_of((1 - core) * rows, 8), rows)
    copies = []
    for k in (1, 2, 3):
        copy = send(result_ref.at[mine], out_ref.at[column, mine], sems, k - 1, peers[k - 1])
        copy.start()
        copies.append(copy)
    out_ref[column] = result_ref[...]
    shared = []
    for k in (1, 2, 3):
        send(result_ref.at[mine], out_ref.at[column ^ k, mine], sems, k - 1, peers[k - 1]).wait_recv()
        copy = send(out_ref.at[column ^ k, mine], out_ref.at[column ^ k, mine], share_sems, k - 1, sibling)
        copy.start()
        shared.append(copy)
    for k in (1, 2, 3):
        part = out_ref.at[column ^ k, other]
        send(part, part, share_sems, k - 1, sibling).wait_recv()
        copies[k - 1].wait_send()
        shared[k - 1].wait_send()


def spread(result):
    vmem = pl.BlockSpec(memory_space=pltpu.VMEM)
    return pl.pallas_call(
        spread_kernel,
        out_shape=jax.ShapeDtypeStruct((4,) + result.shape, result.dtype),
        in_specs=[vmem],
        out_specs=vmem,
        scratch_shapes=[pltpu.SemaphoreType.DMA((2, 3)), pltpu.SemaphoreType.DMA((2, 3))],
        compiler_params=pltpu.CompilerParams(
            collective_id=1, has_side_effects=True, vmem_limit_bytes=16 * 2 ** 20),
    )(result)


def direct_body(line_columns, line_widths, layer_owner):
    total_rows = lax.axis_size("dp") * lax.axis_size("owner") * line_columns.shape[1]
    ends = jnp.cumsum(line_widths[0])
    info = jnp.concatenate([ends - line_widths[0], ends]).astype(jnp.int32)
    info = jnp.broadcast_to(info[:, None], (info.shape[0], tile))
    gram = reduced_gram(line_columns, info)
    return jnp.take(spread(precondition(gram, total_rows)), layer_owner, axis=0)


def solution(mesh):
    in_specs = (P(None, ("dp", "owner"), None), P(("dp", "owner"), None), P())
    chosen = direct_body if dict(mesh.shape) == {"dp": 8, "owner": 4} else body
    return jax.shard_map(chosen, mesh=mesh, in_specs=in_specs, out_specs=P(), check_vma=False)
```

```python
import functools

import jax
import jax.numpy as jnp
from jax import lax
from jax.experimental import pallas as pl
from jax.experimental.pallas import tpu as pltpu
from jax.sharding import PartitionSpec as P

damping = 0.1
tile = 128
HIGHEST = lax.Precision.HIGHEST


def invert_tile(matrix):
    lane = lax.broadcasted_iota(jnp.int32, (8, tile), 1)
    sub = lax.broadcasted_iota(jnp.int32, (8, tile), 0)
    lanes = lax.broadcasted_iota(jnp.int32, (tile, tile), 1)
    for low in range(0, tile, 8):
        rows = matrix[low:low + 8, :]
        unit = jnp.where(lane - low == sub, 1.0, 0.0)
        panel = jnp.where((lane >= low) & (lane < low + 8), unit, rows)
        pivot = [jnp.broadcast_to(rows[:, low + j:low + j + 1], (8, tile)) for j in range(8)]
        for j in range(8):
            inverse = 1.0 / pivot[j][j:j + 1, :]
            for m in range(j + 1, 8):
                scaled = pivot[m][j:j + 1, :] * inverse
                pivot[m] = jnp.where(sub == j, scaled, pivot[m] - pivot[j] * scaled)
            scaled = panel[j:j + 1, :] * inverse
            panel = jnp.where(sub == j, scaled, panel - pivot[j] * scaled)
        total = jnp.where((lanes >= low) & (lanes < low + 8), 0.0, matrix)
        for j in range(8):
            total = total - matrix[:, low + j:low + j + 1] * panel[j:j + 1, :]
        pieces = [total[:low], panel, total[low + 8:]]
        matrix = jnp.concatenate([piece for piece in pieces if piece.shape[0]], axis=0)
    return matrix


def dot(a, b):
    return jnp.dot(a, b, precision=HIGHEST, preferred_element_type=jnp.float32)


triangle = range(3)
needs = [
    [(r, c) for c in range(r, 3)] + [(r, c + 4) for c in range(r, 3)]
    + [(c, r + 4) for c in range(r + 1, 3)] + [(r, 3)] for r in triangle
] + [
    [(r, c + 11) for c in range(r, 3)] + [(r, c + 8) for c in triangle] + [(r, 7)] for r in triangle
] + [
    [(r, c + 14) for c in range(r, 3)] + [(3, r + 4)] for r in triangle
] + [[(3, 3)]]
waves = ((0, 2), (2, 5), (5, 10))
halves, quarters, share, per_wave = 2, 4, 6, 2
place_of = {}
for w, (begin, end) in enumerate(waves):
    for i, t in enumerate([t for need in needs[begin:end] for t in need]):
        place_of[t] = (i // (quarters * per_wave), i // per_wave % quarters, per_wave * w + i % per_wave)


def add_panel(gram_ref, work, scale, p):
    eye = jnp.where(
        lax.broadcasted_iota(jnp.int32, (tile, tile), 0)
        == lax.broadcasted_iota(jnp.int32, (tile, tile), 1), damping, 0.0)

    def gram(r, c):
        h, q, s = place_of[(r, c)]
        return gram_ref[h, q, s] * scale

    def put(c, value):
        work[p * tile:(p + 1) * tile, c * tile:(c + 1) * tile] += value

    if p == 9:
        put(0, gram(3, 3) + eye)
        return
    tap, r = p // 3, p % 3
    for c in range(r, 3):
        centre = gram(r, c) + eye if r == c else gram(r, c)
        if tap:
            centre = centre - gram(r, c + (11 if tap == 1 else 14))
        put(3 * tap + c, centre)
    for c in range(3):
        if tap == 0:
            put(3 + c, gram(c, r + 4).T)
            put(6 + c, gram(r, c + 4))
        if tap == 1:
            put(6 + c, gram(r, c + 8))
    put(9, gram(3, r + 4).T if tap == 2 else gram(r, 7 if tap == 1 else 3))


def eliminate_all(work, solved, prepare):
    blocks = 9

    def eliminate(j, carry):
        prepare(j)
        top = pl.ds(pl.multiple_of(j * tile, tile), tile)
        col = pl.multiple_of(jnp.where(j == blocks, 0, j) * tile, tile)
        inverse = invert_tile(work[top, pl.ds(col, tile)])

        @pl.when(j < blocks)
        def _():
            row = dot(inverse, work[top, :])
            solved[top, :] = row

            def update(i, carry):
                where = pl.ds(pl.multiple_of(i * tile, tile), tile)
                work[where, :] -= dot(work[top, where].T, solved[top, :])
                return carry

            lax.fori_loop(j + 1, blocks, update, 0)

        @pl.when(j == blocks)
        def _():
            solved[top, 0:tile] = inverse

        return carry

    lax.fori_loop(0, blocks + 1, eliminate, 0)


def substitute(solved, answer, tap):
    n = 9 * tile
    for j in range(3 * tap + 2, 3 * tap - 1, -1):
        rows = slice(j * tile, (j + 1) * tile)
        value = solved[rows, n:n + tile]
        if j < 8:
            after = slice((j + 1) * tile, n)
            value = value - dot(solved[rows, after], answer[after, :])
        answer[rows, :] = value
    rows = slice(3 * tap * tile, 3 * (tap + 1) * tile)
    return dot(answer[rows, :], solved[n:n + tile, 0:tile]), (1, 0, 2)[tap] * 3 * tile


def solve_kernel(scale, gram_ref, out_ref, work, solved, answer):
    work[...] = jnp.zeros_like(work)
    for p in range(10):
        add_panel(gram_ref, work, scale, p)
    eliminate_all(work, solved, lambda j: None)
    for tap in (2, 1, 0):
        value, at = substitute(solved, answer, tap)
        out_ref[at:at + 3 * tile, :] = value


def precondition(gram, total_rows):
    n = 9 * tile
    return pl.pallas_call(
        functools.partial(solve_kernel, 1.0 / total_rows),
        out_shape=jax.ShapeDtypeStruct((n, tile), jnp.float32),
        in_specs=[pl.BlockSpec(memory_space=pltpu.VMEM)],
        out_specs=pl.BlockSpec(memory_space=pltpu.VMEM),
        scratch_shapes=[
            pltpu.VMEM((n + tile, n + tile), jnp.float32),
            pltpu.VMEM((n + tile, n + tile), jnp.float32),
            pltpu.VMEM((n, tile), jnp.float32),
        ],
        compiler_params=pltpu.CompilerParams(vmem_limit_bytes=48 * 2 ** 20),
    )(gram)


def pack_tiles(gram):
    filled = {at: gram[r * tile:(r + 1) * tile, c * tile:(c + 1) * tile] for (r, c), at in place_of.items()}
    empty = jnp.zeros((tile, tile), gram.dtype)
    parts = [filled.get((h, q, s), empty)
             for h in range(halves) for q in range(quarters) for s in range(share)]
    return jnp.stack(parts).reshape(halves, quarters, share, tile, tile)


def line_masks(widths, positions):
    ends = jnp.cumsum(widths, axis=-1).astype(jnp.int32)
    starts = ends - widths
    place = jnp.arange(positions, dtype=jnp.int32)[:, None]
    inside = place < ends[..., None, -1:]
    opening = jnp.any(place == starts[..., None, :], axis=-1, keepdims=True)
    closing = jnp.any(place + 1 == ends[..., None, :], axis=-1, keepdims=True)
    return inside, opening, closing


def shifted(block):
    return jnp.concatenate([block[..., 1:, :], jnp.zeros_like(block[..., :1, :])], axis=-2)


def body(line_columns, line_widths, layer_owner):
    layer_count, positions, packed = line_columns.shape
    ch = packed // 4
    feat = 3 * ch
    n_replicas = lax.axis_size("dp")
    n_owners = lax.axis_size("owner")
    total_rows = n_replicas * n_owners * positions
    ordered = jnp.take(line_columns, layer_owner, axis=0)
    width_copies = jnp.broadcast_to(line_widths[None, :, :], (n_owners, 1, line_widths.shape[1]))
    received = lax.all_to_all(ordered, "owner", split_axis=0, concat_axis=1, tiled=True)
    source_widths = lax.all_to_all(width_copies, "owner", split_axis=0, concat_axis=1, tiled=True)
    blocks = received.reshape(n_owners, positions, packed)
    inside, opening, closing = line_masks(source_widths.reshape(n_owners, -1), positions)
    zero = jnp.zeros((), blocks.dtype)
    live = jnp.where(inside, blocks, zero)
    ahead = jnp.where(closing, zero, shifted(live))
    ahead2 = jnp.where(closing, zero, shifted(ahead[..., :feat]))
    last = jnp.where(closing, live[..., :feat], zero)
    start = jnp.where(opening & inside, live[..., :feat], zero)
    right = jnp.concatenate([live, ahead, ahead2, last, start], axis=-1)
    gram = lax.dot_general(
        live.reshape(-1, packed), right.reshape(n_owners * positions, -1),
        (((0,), (0,)), ((), ())), preferred_element_type=jnp.float32)
    gram = lax.psum(pack_tiles(gram), "dp")
    result = precondition(gram, total_rows)
    return lax.all_gather(result[None], "owner", axis=0, tiled=True)


def device(column, core, z):
    return {"dp": 2 * column + core, "owner": z}


def send(src, dst, sems, slot, to):
    return pltpu.make_async_remote_copy(
        src_ref=src, dst_ref=dst, send_sem=sems.at[0, slot], recv_sem=sems.at[1, slot],
        device_id=to, device_id_type=pl.DeviceIdType.MESH)


def here():
    index = lax.axis_index("dp")
    return index // 2, index % 2, lax.axis_index("owner")


def greet(partners):
    barrier = pltpu.get_barrier_semaphore()
    for partner in partners:
        pl.semaphore_signal(barrier, inc=1, device_id=partner, device_id_type=pl.DeviceIdType.MESH)
    return barrier


def block_products(rows_ref, info_ref, gram, first):
    positions, packed = rows_ref.shape
    feat = packed // 4 * 3
    place = lax.broadcasted_iota(jnp.int32, (positions, tile), 0)
    info = info_ref[...]
    lines = info.shape[0] // 2

    def any_of(rows, at):
        hit = at == info[rows[0]:rows[0] + 1, :]
        for r in rows[1:]:
            hit = hit | (at == info[r:r + 1, :])
        return hit

    inside = place < info[2 * lines - 1:2 * lines, :]
    opening = any_of(range(lines), place) & inside
    closing = any_of(range(lines, 2 * lines), place + 1)

    def mask(flag, width):
        return jnp.tile(jnp.where(flag, 1.0, 0.0), (1, width // tile))

    def up(value):
        return pltpu.roll(value, positions - 1, 0)

    inner = mask(inside & ~closing, packed)
    live = rows_ref[...].astype(jnp.float32) * mask(inside, packed)
    ahead = up(live) * inner
    ahead2 = up(ahead[:, :feat]) * inner[:, :feat]
    last = live[:, :feat] * mask(closing, feat)
    start = live[:, :feat] * mask(opening, feat)
    left = live.astype(jnp.bfloat16).T
    at = 0
    for part in (live, ahead, ahead2, last, start):
        cols = slice(at, at + part.shape[1])
        product = jnp.dot(left, part.astype(jnp.bfloat16), preferred_element_type=jnp.float32)
        if first:
            gram[:, cols] = product
        else:
            gram[:, cols] += product
        at += part.shape[1]


def reduce_kernel(rows_ref, info_ref, mine, rows_in, info_in, gram, part, core_in, acc,
                  right_out, left_out, right_in, left_in,
                  row_sems, info_sems, core_sems, right_sems, left_sems):
    column, core, z = here()
    top = quarters - 1
    peers = [device(column ^ k, core, z) for k in (1, 2, 3)]
    sibling = device(column, 1 - core, z)
    right, left = device(column, core, z + 1), device(column, core, z - 1)
    barrier = greet(peers + [sibling])

    @pl.when(z < top)
    def _():
        pl.semaphore_signal(barrier, inc=1, device_id=right, device_id_type=pl.DeviceIdType.MESH)

    @pl.when(z > 0)
    def _():
        pl.semaphore_signal(barrier, inc=1, device_id=left, device_id_type=pl.DeviceIdType.MESH)

    pl.semaphore_wait(barrier, 4 + jnp.where(z < top, 1, 0) + jnp.where(z > 0, 1, 0))

    rows_out = []
    for k in (1, 2, 3):
        note = send(info_ref, info_in.at[k - 1], info_sems, k - 1, peers[k - 1])
        note.start()
        copy = send(rows_ref.at[column ^ k], rows_in.at[k - 1], row_sems, k - 1, peers[k - 1])
        copy.start()
        rows_out.append((note, copy))
    block_products(rows_ref.at[column], info_ref, gram, True)
    for k in (1, 2, 3):
        for copy in rows_out[k - 1]:
            copy.wait_recv()
        block_products(rows_in.at[k - 1], info_in.at[k - 1], gram, False)

    for t, (h, q, s) in place_of.items():
        r, c = t
        part[h, q, s] = gram[r * tile:(r + 1) * tile, c * tile:(c + 1) * tile]
    for h in range(halves):
        for q in range(quarters):
            for s in range(share):
                if (h, q, s) not in place_of.values():
                    part[h, q, s] = jnp.zeros((tile, tile), jnp.float32)

    order = (3, 0, 2, 1)
    core_out = {}
    for q in order:
        core_out[q] = send(part.at[1 - core, q], core_in.at[q], core_sems, q, sibling)
        core_out[q].start()
    for q in order:
        core_out[q].wait_recv()
        acc[q] = part[core, q] + core_in[q]

    def hop(q, out, into, sems, to):
        return send(out.at[q], into.at[q], sems, q, to)

    for step in range(top):
        for q, out, into, sems, to, sends, first in (
            (top - step, right_out, right_in, right_sems, right, z < top - step, z == 0),
            (step, left_out, left_in, left_sems, left, z > step, z == top),
        ):
            takes = (z > 0) & (z <= q) if out is right_out else (z < top) & (z >= q)
            copy = hop(q, out, into, sems, to)

            @pl.when(takes)
            def _(copy=copy):
                copy.wait_recv()

            @pl.when(sends & first)
            def _(copy=copy, q=q, out=out):
                out[q] = acc[q]
                copy.start()

            @pl.when(sends & ~first)
            def _(copy=copy, q=q, out=out, into=into):
                out[q] = acc[q] + into[q]
                copy.start()

    mine[...] = acc[z]

    @pl.when(z > 0)
    def _():
        mine[...] += right_in[z]

    @pl.when(z < top)
    def _():
        mine[...] += left_in[z]

    for pair in rows_out:
        for copy in pair:
            copy.wait_send()
    for q in range(quarters):
        core_out[q].wait_send()

        @pl.when(z < q)
        def _(q=q):
            hop(q, right_out, right_in, right_sems, right).wait_send()

        @pl.when(z > q)
        def _(q=q):
            hop(q, left_out, left_in, left_sems, left).wait_send()


def reduced_quarter(rows, info):
    columns, positions, packed = rows.shape
    wide = 4 * packed + tile
    quarter = (quarters, share, tile, tile)
    vmem = pl.BlockSpec(memory_space=pltpu.VMEM)
    return pl.pallas_call(
        reduce_kernel,
        out_shape=jax.ShapeDtypeStruct(quarter[1:], jnp.float32),
        in_specs=[vmem, vmem],
        out_specs=vmem,
        scratch_shapes=[
            pltpu.VMEM((3, positions, packed), rows.dtype),
            pltpu.VMEM((3,) + info.shape, info.dtype),
            pltpu.VMEM((packed, wide), jnp.float32),
            pltpu.VMEM((halves,) + quarter, jnp.float32),
        ] + [pltpu.VMEM(quarter, jnp.float32)] * 6 + [
            pltpu.SemaphoreType.DMA((2, 3)),
            pltpu.SemaphoreType.DMA((2, 3)),
        ] + [pltpu.SemaphoreType.DMA((2, quarters))] * 3,
        compiler_params=pltpu.CompilerParams(
            collective_id=0, has_side_effects=True, vmem_limit_bytes=48 * 2 ** 20),
    )(rows, info)


def finish_kernel(scale, mine, out_ref, full, work, solved, answer,
                  give_sems, share_sems, row_sems, pass_sems):
    column, core, z = here()
    peers = [device(column ^ k, core, z) for k in (1, 2, 3)]
    chain = [device(column, core, z ^ k) for k in (1, 2, 3)]
    sibling = device(column, 1 - core, z)
    barrier = greet(peers + chain + [sibling])
    full[core, z] = mine[...]
    work[...] = jnp.zeros_like(work)
    pl.semaphore_wait(barrier, 7)

    def piece(h, q, w):
        return full.at[h, q, pl.ds(per_wave * w, per_wave)]

    def give(w, k):
        return send(piece(core, z, w), piece(core, z, w), give_sems, 3 * w + k - 1, chain[k - 1])

    def arriving(w, k):
        return send(piece(core, z ^ k, w), piece(core, z ^ k, w), give_sems, 3 * w + k - 1, chain[k - 1])

    def share_piece(h, w, k):
        return send(piece(h, z ^ k, w), piece(h, z ^ k, w), share_sems, 4 * w + k, sibling)

    def begin(w):
        for k in (3, 2, 1):
            give(w, k).start()
        share_piece(core, w, 0).start()

    begin(0)

    def prepare(j):
        for w, (first, end) in enumerate(waves):
            @pl.when(j == first)
            def _(w=w, first=first, end=end):
                for k in (1, 2, 3):
                    arriving(w, k).wait_recv()
                    share_piece(core, w, k).start()
                if w + 1 < len(waves):
                    begin(w + 1)
                for k in range(4):
                    share_piece(1 - core, w, k).wait_recv()
                for p in range(first, end):
                    add_panel(full, work, scale, p)

    eliminate_all(work, solved, prepare)

    half = 3 * tile // 2

    def rows_of(col, side, at):
        return out_ref.at[col, pl.ds(pl.multiple_of(at + side * half, 8), half)]

    def spread_rows(at, tap, k):
        part = rows_of(column, core, at)
        return send(part, part, row_sems, 3 * tap + k - 1, peers[k - 1])

    def pass_rows(side, at, tap, k):
        part = rows_of(column ^ k, side, at)
        return send(part, part, pass_sems, 3 * tap + k - 1, sibling)

    order = []
    for tap in (2, 1, 0):
        value, at = substitute(solved, answer, tap)
        out_ref[column, at:at + 3 * tile, :] = value
        for k in (1, 2, 3):
            spread_rows(at, tap, k).start()
        order.append((at, tap))
    for at, tap in order:
        for k in (1, 2, 3):
            part = rows_of(column ^ k, core, at)
            send(part, part, row_sems, 3 * tap + k - 1, peers[k - 1]).wait_recv()
            pass_rows(core, at, tap, k).start()
    for at, tap in order:
        for k in (1, 2, 3):
            pass_rows(1 - core, at, tap, k).wait_recv()
            pass_rows(core, at, tap, k).wait_send()
            spread_rows(at, tap, k).wait_send()
    for w in range(len(waves)):
        for k in (1, 2, 3):
            give(w, k).wait_send()
        for k in range(4):
            share_piece(core, w, k).wait_send()


def finish(mine, total_rows):
    vmem = pl.BlockSpec(memory_space=pltpu.VMEM)
    n = 9 * tile
    return pl.pallas_call(
        functools.partial(finish_kernel, 1.0 / total_rows),
        out_shape=jax.ShapeDtypeStruct((4, n, tile), mine.dtype),
        in_specs=[vmem],
        out_specs=vmem,
        scratch_shapes=[
            pltpu.VMEM((halves, quarters, share, tile, tile), jnp.float32),
            pltpu.VMEM((n + tile, n + tile), jnp.float32),
            pltpu.VMEM((n + tile, n + tile), jnp.float32),
            pltpu.VMEM((n, tile), jnp.float32),
            pltpu.SemaphoreType.DMA((2, 9)),
            pltpu.SemaphoreType.DMA((2, 12)),
            pltpu.SemaphoreType.DMA((2, 9)),
            pltpu.SemaphoreType.DMA((2, 9)),
        ],
        compiler_params=pltpu.CompilerParams(
            collective_id=1, has_side_effects=True, vmem_limit_bytes=48 * 2 ** 20),
    )(mine)


def direct_body(line_columns, line_widths, layer_owner):
    total_rows = lax.axis_size("dp") * lax.axis_size("owner") * line_columns.shape[1]
    ends = jnp.cumsum(line_widths[0])
    info = jnp.concatenate([ends - line_widths[0], ends]).astype(jnp.int32)
    info = jnp.broadcast_to(info[:, None], (info.shape[0], tile))
    mine = reduced_quarter(line_columns, info)
    return jnp.take(finish(mine, total_rows), layer_owner, axis=0)


def solution(mesh):
    in_specs = (P(None, ("dp", "owner"), None), P(("dp", "owner"), None), P())
    chosen = direct_body if dict(mesh.shape) == {"dp": 8, "owner": 4} else body
    return jax.shard_map(chosen, mesh=mesh, in_specs=in_specs, out_specs=P(), check_vma=False)
```

```python
import functools

import jax
import jax.numpy as jnp
from jax import lax
from jax.experimental import pallas as pl
from jax.experimental.pallas import tpu as pltpu
from jax.sharding import PartitionSpec as P

damping = 0.1
tile = 128
HIGHEST = lax.Precision.HIGHEST


def invert_tile(matrix):
    lane = lax.broadcasted_iota(jnp.int32, (8, tile), 1)
    sub = lax.broadcasted_iota(jnp.int32, (8, tile), 0)
    lanes = lax.broadcasted_iota(jnp.int32, (tile, tile), 1)
    for low in range(0, tile, 8):
        rows = matrix[low:low + 8, :]
        unit = jnp.where(lane - low == sub, 1.0, 0.0)
        panel = jnp.where((lane >= low) & (lane < low + 8), unit, rows)
        pivot = [jnp.broadcast_to(rows[:, low + j:low + j + 1], (8, tile)) for j in range(8)]
        for j in range(8):
            inverse = 1.0 / pivot[j][j:j + 1, :]
            for m in range(j + 1, 8):
                scaled = pivot[m][j:j + 1, :] * inverse
                pivot[m] = jnp.where(sub == j, scaled, pivot[m] - pivot[j] * scaled)
            scaled = panel[j:j + 1, :] * inverse
            panel = jnp.where(sub == j, scaled, panel - pivot[j] * scaled)
        total = jnp.where((lanes >= low) & (lanes < low + 8), 0.0, matrix)
        for j in range(8):
            total = total - matrix[:, low + j:low + j + 1] * panel[j:j + 1, :]
        pieces = [total[:low], panel, total[low + 8:]]
        matrix = jnp.concatenate([piece for piece in pieces if piece.shape[0]], axis=0)
    return matrix


def dot(a, b):
    return jnp.dot(a, b, precision=HIGHEST, preferred_element_type=jnp.float32)


triangle = range(3)
tiles = [(3, 3)]
for r in triangle:
    tiles += [(r, c) for c in range(r, 3)] + [(r, c + 4) for c in range(r, 3)]
    tiles += [(c, r + 4) for c in range(r + 1, 3)] + [(r, 3)]
for r in triangle:
    tiles += [(r, c + 8) for c in triangle] + [(r, 7)]
tiles += [(3, r + 4) for r in triangle]
halves, quarters, slots = 2, 4, 4
parts = halves * quarters
strip = tile // quarters
share = slots * tile + strip
wave_rows = ((0, 2 * tile), (2 * tile, share))
strips_of = {}
for i, t in enumerate(tiles):
    if i < parts * slots:
        w, k = divmod(i, 2 * parts)
        strips_of[t] = [(k // 8, k // 2 % 4, (2 * w + k % 2) * tile, tile)]
    else:
        strips_of[t] = [(i - parts * slots, q, slots * tile, strip) for q in range(quarters)]


def read_tile(gram_ref, t):
    pieces = [gram_ref[h, q, at:at + rows, :] for h, q, at, rows in strips_of[t]]
    return pieces[0] if len(pieces) == 1 else jnp.concatenate(pieces, axis=0)


def add_panel(gram_ref, edge_ref, work, scale, p):
    eye = jnp.where(
        lax.broadcasted_iota(jnp.int32, (tile, tile), 0)
        == lax.broadcasted_iota(jnp.int32, (tile, tile), 1), damping, 0.0)

    def gram(r, c):
        return read_tile(gram_ref, (r, c)) * scale

    def put(c, value):
        work[p * tile:(p + 1) * tile, c * tile:(c + 1) * tile] += value

    if p == 9:
        put(0, gram(3, 3) + eye)
        return
    tap, r = p // 3, p % 3
    for c in range(r, 3):
        centre = gram(r, c) + eye if r == c else gram(r, c)
        if tap:
            edge = edge_ref[2 - tap, r * tile:(r + 1) * tile, c * tile:(c + 1) * tile]
            centre = centre - edge * scale
        put(3 * tap + c, centre)
    for c in range(3):
        if tap == 0:
            put(3 + c, gram(c, r + 4).T)
            put(6 + c, gram(r, c + 4))
        if tap == 1:
            put(6 + c, gram(r, c + 8))
    put(9, gram(3, r + 4).T if tap == 2 else gram(r, 7 if tap == 1 else 3))


def eliminate_all(work, solved, prepare):
    blocks, n = 9, 9 * tile

    def block(i):
        return slice(i * tile, (i + 1) * tile)

    inverse = invert_tile(work[block(0), block(0)])
    solved[n:n + tile, 0:tile] = invert_tile(work[block(blocks), block(0)])
    for j in range(blocks):
        prepare(j)
        row = work[block(j), :]
        if j + 1 < blocks:
            ahead = row[:, block(j + 1)].T
            corner = work[block(j + 1), block(j + 1)] - dot(ahead, dot(inverse, row[:, block(j + 1)]))
            following = invert_tile(corner)
        right = dot(inverse, row[:, (j + 1) * tile:])
        solved[block(j), (j + 1) * tile:] = right
        for i in range(j + 1, blocks):
            work[block(i), i * tile:] -= dot(row[:, block(i)].T, right[:, (i - j - 1) * tile:])
        if j + 1 < blocks:
            inverse = following


def substitute(solved, answer, tap):
    n = 9 * tile
    for j in range(3 * tap + 2, 3 * tap - 1, -1):
        rows = slice(j * tile, (j + 1) * tile)
        value = solved[rows, n:n + tile]
        if j < 8:
            after = slice((j + 1) * tile, n)
            value = value - dot(solved[rows, after], answer[after, :])
        answer[rows, :] = value
    rows = slice(3 * tap * tile, 3 * (tap + 1) * tile)
    return dot(answer[rows, :], solved[n:n + tile, 0:tile]), (1, 0, 2)[tap] * 3 * tile


def solve_kernel(scale, gram_ref, edge_ref, out_ref, work, solved, answer):
    work[...] = jnp.zeros_like(work)
    for p in range(10):
        add_panel(gram_ref, edge_ref, work, scale, p)
    eliminate_all(work, solved, lambda j: None)
    for tap in (2, 1, 0):
        value, at = substitute(solved, answer, tap)
        out_ref[at:at + 3 * tile, :] = value


def precondition(gram, edges, total_rows):
    n = 9 * tile
    return pl.pallas_call(
        functools.partial(solve_kernel, 1.0 / total_rows),
        out_shape=jax.ShapeDtypeStruct((n, tile), jnp.float32),
        in_specs=[pl.BlockSpec(memory_space=pltpu.VMEM)] * 2,
        out_specs=pl.BlockSpec(memory_space=pltpu.VMEM),
        scratch_shapes=[
            pltpu.VMEM((n + tile, n + tile), jnp.float32),
            pltpu.VMEM((n + tile, n + tile), jnp.float32),
            pltpu.VMEM((n, tile), jnp.float32),
        ],
        compiler_params=pltpu.CompilerParams(vmem_limit_bytes=48 * 2 ** 20),
    )(gram, edges)


def pack_tiles(gram):
    pieces = {}
    for r, c in tiles:
        start = r * tile
        for h, q, at, rows in strips_of[(r, c)]:
            pieces[(h, q, at)] = gram[start:start + rows, c * tile:(c + 1) * tile]
            start += rows
    return jnp.concatenate([pieces[key] for key in sorted(pieces)]).reshape(halves, quarters, share, tile)


def line_masks(widths, positions):
    ends = jnp.cumsum(widths, axis=-1).astype(jnp.int32)
    starts = ends - widths
    place = jnp.arange(positions, dtype=jnp.int32)[:, None]
    inside = place < ends[..., None, -1:]
    opening = jnp.any(place == starts[..., None, :], axis=-1, keepdims=True)
    closing = jnp.any(place + 1 == ends[..., None, :], axis=-1, keepdims=True)
    return inside, opening, closing


def shifted(block):
    return jnp.concatenate([block[..., 1:, :], jnp.zeros_like(block[..., :1, :])], axis=-2)


def body(line_columns, line_widths, layer_owner):
    layer_count, positions, packed = line_columns.shape
    ch = packed // 4
    feat = 3 * ch
    n_replicas = lax.axis_size("dp")
    n_owners = lax.axis_size("owner")
    total_rows = n_replicas * n_owners * positions
    ordered = jnp.take(line_columns, layer_owner, axis=0)
    width_copies = jnp.broadcast_to(line_widths[None, :, :], (n_owners, 1, line_widths.shape[1]))
    received = lax.all_to_all(ordered, "owner", split_axis=0, concat_axis=1, tiled=True)
    source_widths = lax.all_to_all(width_copies, "owner", split_axis=0, concat_axis=1, tiled=True)
    blocks = received.reshape(n_owners, positions, packed)
    inside, opening, closing = line_masks(source_widths.reshape(n_owners, -1), positions)
    zero = jnp.zeros((), blocks.dtype)
    live = jnp.where(inside, blocks, zero)
    ahead = jnp.where(closing, zero, shifted(live))
    ahead2 = jnp.where(closing, zero, shifted(ahead[..., :feat]))
    last = jnp.where(closing, live[..., :feat], zero)
    start = jnp.where(opening & inside, live[..., :feat], zero)
    right = jnp.concatenate([live, ahead, ahead2], axis=-1)
    gram = lax.dot_general(
        live.reshape(-1, packed), right.reshape(n_owners * positions, -1),
        (((0,), (0,)), ((), ())), preferred_element_type=jnp.float32)
    ends = jnp.stack([start, last]).reshape(2, n_owners * positions, feat)
    edges = jnp.einsum("srp,srq->spq", ends, ends, preferred_element_type=jnp.float32)
    result = precondition(lax.psum(pack_tiles(gram), "dp"), lax.psum(edges, "dp"), total_rows)
    return lax.all_gather(result[None], "owner", axis=0, tiled=True)


def device(column, core, z):
    return {"dp": 2 * column + core, "owner": z}


def send(src, dst, sems, slot, to):
    return pltpu.make_async_remote_copy(
        src_ref=src, dst_ref=dst, send_sem=sems.at[0, slot], recv_sem=sems.at[1, slot],
        device_id=to, device_id_type=pl.DeviceIdType.MESH)


def here():
    index = lax.axis_index("dp")
    return index // 2, index % 2, lax.axis_index("owner")


def greet(partners):
    barrier = pltpu.get_barrier_semaphore()
    for partner in partners:
        pl.semaphore_signal(barrier, inc=1, device_id=partner, device_id_type=pl.DeviceIdType.MESH)
    return barrier


def block_products(rows_ref, info_ref, gram, edges, index):
    positions, packed = rows_ref.shape
    feat = packed // 4 * 3
    place = lax.broadcasted_iota(jnp.int32, (positions, tile), 0)
    info = info_ref[...]
    lines = info.shape[0] // 2

    def any_of(rows, at):
        hit = at == info[rows[0]:rows[0] + 1, :]
        for r in rows[1:]:
            hit = hit | (at == info[r:r + 1, :])
        return hit

    inside = place < info[2 * lines - 1:2 * lines, :]
    closing = any_of(range(lines, 2 * lines), place + 1)

    def mask(flag, width):
        return jnp.tile(jnp.where(flag, 1.0, 0.0), (1, width // tile))

    def up(value):
        return pltpu.roll(value, positions - 1, 0)

    inner = mask(inside & ~closing, packed)
    live = rows_ref[...].astype(jnp.float32) * mask(inside, packed)
    ahead = up(live) * inner
    ahead2 = up(ahead[:, :feat]) * inner[:, :feat]
    live_low = live.astype(jnp.bfloat16)
    wanted = info[:, 0:1] - jnp.where(lax.broadcasted_iota(jnp.int32, (2 * lines, 1), 0) < lines, 0, 1)
    pick = jnp.where(lax.broadcasted_iota(jnp.int32, (2 * lines, positions), 1) == wanted, 1.0, 0.0)
    picked = jnp.dot(pick.astype(jnp.bfloat16), live_low[:, :feat], preferred_element_type=jnp.float32)
    edges[0, lines * index:lines * (index + 1), :] = picked[:lines]
    edges[1, lines * index:lines * (index + 1), :] = picked[lines:]
    left = live_low.T
    at = 0
    for part in (live, ahead, ahead2):
        cols = slice(at, at + part.shape[1])
        product = jnp.dot(left, part.astype(jnp.bfloat16), preferred_element_type=jnp.float32)
        if index == 0:
            gram[:, cols] = product
        else:
            gram[:, cols] += product
        at += part.shape[1]


def reduce_kernel(rows_ref, info_ref, mine, edge_out, rows_in, info_in, gram, edges, part, core_in, acc,
                  right_out, left_out, right_in, left_in,
                  row_sems, info_sems, core_sems, right_sems, left_sems):
    column, core, z = here()
    top = quarters - 1
    peers = [device(column ^ k, core, z) for k in (1, 2, 3)]
    sibling = device(column, 1 - core, z)
    right, left = device(column, core, z + 1), device(column, core, z - 1)
    barrier = greet(peers + [sibling])

    @pl.when(z < top)
    def _():
        pl.semaphore_signal(barrier, inc=1, device_id=right, device_id_type=pl.DeviceIdType.MESH)

    @pl.when(z > 0)
    def _():
        pl.semaphore_signal(barrier, inc=1, device_id=left, device_id_type=pl.DeviceIdType.MESH)

    pl.semaphore_wait(barrier, 4 + jnp.where(z < top, 1, 0) + jnp.where(z > 0, 1, 0))

    rows_out = []
    for k in (1, 2, 3):
        note = send(info_ref, info_in.at[k - 1], info_sems, k - 1, peers[k - 1])
        note.start()
        copy = send(rows_ref.at[column ^ k], rows_in.at[k - 1], row_sems, k - 1, peers[k - 1])
        copy.start()
        rows_out.append((note, copy))
    block_products(rows_ref.at[column], info_ref, gram, edges, 0)
    for k in (1, 2, 3):
        for copy in rows_out[k - 1]:
            copy.wait_recv()
        block_products(rows_in.at[k - 1], info_in.at[k - 1], gram, edges, k)

    for r, c in tiles:
        start = r * tile
        for h, q, at, rows in strips_of[(r, c)]:
            part[h, q, at:at + rows, :] = gram[start:start + rows, c * tile:(c + 1) * tile]
            start += rows
    edge_out[...] = edges[...].astype(edge_out.dtype)

    order = (3, 0, 2, 1)
    core_out = {}
    for q in order:
        core_out[q] = send(part.at[1 - core, q], core_in.at[q], core_sems, q, sibling)
        core_out[q].start()
    for q in order:
        core_out[q].wait_recv()
        acc[q] = part[core, q] + core_in[q]

    def hop(q, out, into, sems, to):
        return send(out.at[q], into.at[q], sems, q, to)

    for step in range(top):
        for q, out, into, sems, to, sends, first in (
            (top - step, right_out, right_in, right_sems, right, z < top - step, z == 0),
            (step, left_out, left_in, left_sems, left, z > step, z == top),
        ):
            takes = (z > 0) & (z <= q) if out is right_out else (z < top) & (z >= q)
            copy = hop(q, out, into, sems, to)

            @pl.when(takes)
            def _(copy=copy):
                copy.wait_recv()

            @pl.when(sends & first)
            def _(copy=copy, q=q, out=out):
                out[q] = acc[q]
                copy.start()

            @pl.when(sends & ~first)
            def _(copy=copy, q=q, out=out, into=into):
                out[q] = acc[q] + into[q]
                copy.start()

    mine[...] = acc[z]

    @pl.when(z > 0)
    def _():
        mine[...] += right_in[z]

    @pl.when(z < top)
    def _():
        mine[...] += left_in[z]

    for pair in rows_out:
        for copy in pair:
            copy.wait_send()
    for q in range(quarters):
        core_out[q].wait_send()

        @pl.when(z < q)
        def _(q=q):
            hop(q, right_out, right_in, right_sems, right).wait_send()

        @pl.when(z > q)
        def _(q=q):
            hop(q, left_out, left_in, left_sems, left).wait_send()


def reduced_part(rows, info):
    columns, positions, packed = rows.shape
    feat = packed // 4 * 3
    edge_shape = (2, info.shape[0] // 2 * columns, feat)
    quarter = (quarters, share, tile)
    vmem = pl.BlockSpec(memory_space=pltpu.VMEM)
    return pl.pallas_call(
        reduce_kernel,
        out_shape=[
            jax.ShapeDtypeStruct(quarter[1:], jnp.float32),
            jax.ShapeDtypeStruct(edge_shape, rows.dtype),
        ],
        in_specs=[vmem, vmem],
        out_specs=[vmem, vmem],
        scratch_shapes=[
            pltpu.VMEM((3, positions, packed), rows.dtype),
            pltpu.VMEM((3,) + info.shape, info.dtype),
            pltpu.VMEM((packed, 2 * packed + feat), jnp.float32),
            pltpu.VMEM(edge_shape, jnp.float32),
            pltpu.VMEM((halves,) + quarter, jnp.float32),
        ] + [pltpu.VMEM(quarter, jnp.float32)] * 6 + [
            pltpu.SemaphoreType.DMA((2, 3)),
            pltpu.SemaphoreType.DMA((2, 3)),
        ] + [pltpu.SemaphoreType.DMA((2, quarters))] * 3,
        compiler_params=pltpu.CompilerParams(
            collective_id=0, has_side_effects=True, vmem_limit_bytes=48 * 2 ** 20),
    )(rows, info)


def finish_kernel(scale, mine, ends_ref, out_ref, full, ends, edges, work, solved, answer,
                  give_sems, share_sems, end_sems, row_sems, pass_sems):
    column, core, z = here()
    peers = [device(column ^ k, core, z) for k in (1, 2, 3)]
    chain = [device(column, core, z ^ k) for k in (1, 2, 3)]
    sibling = device(column, 1 - core, z)
    across = [device(column, 1 - core, z ^ k) for k in (1, 2, 3)]
    barrier = greet(peers + chain + [sibling] + across)
    full[core, z] = mine[...]
    place = 2 * z + core
    ends[place] = ends_ref[...]
    work[...] = jnp.zeros_like(work)
    pl.semaphore_wait(barrier, 10)

    def piece(h, q, w):
        first, end = wave_rows[w]
        return full.at[h, q, pl.ds(first, end - first)]

    def give(w, k):
        return send(piece(core, z, w), piece(core, z, w), give_sems, 3 * w + k - 1, chain[k - 1])

    def arriving(w, k):
        return send(piece(core, z ^ k, w), piece(core, z ^ k, w), give_sems, 3 * w + k - 1, chain[k - 1])

    def share_piece(h, w, k):
        return send(piece(h, z ^ k, w), piece(h, z ^ k, w), share_sems, 4 * w + k, sibling)

    def begin(w):
        for k in (3, 2, 1):
            give(w, k).start()
        share_piece(core, w, 0).start()

    def arrive(w):
        for k in (1, 2, 3):
            arriving(w, k).wait_recv()
            share_piece(core, w, k).start()

    def shared(w):
        for k in range(4):
            share_piece(1 - core, w, k).wait_recv()

    column_mates = [(sibling, 0, 1)] + [
        (chain[k - 1], k, 0) for k in (1, 2, 3)] + [(across[k - 1], k, 1) for k in (1, 2, 3)]

    def end_rows(index, arrived):
        to, k, flip = column_mates[index]
        at = 2 * (z ^ k) + (1 - core if flip else core) if arrived else place
        return send(ends.at[at], ends.at[at], end_sems, index, to)

    begin(0)
    for index in range(len(column_mates)):
        end_rows(index, False).start()
    arrive(0)
    begin(1)
    shared(0)
    for p in (9, 0, 1):
        add_panel(full, edges, work, scale, p)

    def prepare(j):
        if j == 1:
            arrive(1)
            for index in range(len(column_mates)):
                end_rows(index, True).wait_recv()
            for side in range(2):
                rows = ends[:, side].reshape(-1, ends.shape[-1])
                edges[side] = jnp.dot(rows.T, rows, preferred_element_type=jnp.float32)
            shared(1)
            for p in range(2, 9):
                add_panel(full, edges, work, scale, p)

    eliminate_all(work, solved, prepare)

    half = 3 * tile // 2

    def rows_of(col, side, at):
        return out_ref.at[col, pl.ds(pl.multiple_of(at + side * half, 8), half)]

    def spread_rows(at, tap, k):
        part = rows_of(column, core, at)
        return send(part, part, row_sems, 3 * tap + k - 1, peers[k - 1])

    def pass_rows(side, at, tap, k):
        part = rows_of(column ^ k, side, at)
        return send(part, part, pass_sems, 3 * tap + k - 1, sibling)

    order = []
    for tap in (2, 1, 0):
        value, at = substitute(solved, answer, tap)
        out_ref[column, at:at + 3 * tile, :] = value
        for k in (1, 2, 3):
            spread_rows(at, tap, k).start()
        order.append((at, tap))
    for at, tap in order:
        for k in (1, 2, 3):
            part = rows_of(column ^ k, core, at)
            send(part, part, row_sems, 3 * tap + k - 1, peers[k - 1]).wait_recv()
            pass_rows(core, at, tap, k).start()
    for at, tap in order:
        for k in (1, 2, 3):
            pass_rows(1 - core, at, tap, k).wait_recv()
            pass_rows(core, at, tap, k).wait_send()
            spread_rows(at, tap, k).wait_send()
    for w in range(len(wave_rows)):
        for k in (1, 2, 3):
            give(w, k).wait_send()
        for k in range(4):
            share_piece(core, w, k).wait_send()
    for index in range(len(column_mates)):
        end_rows(index, False).wait_send()


def finish(mine, ends, total_rows):
    vmem = pl.BlockSpec(memory_space=pltpu.VMEM)
    n = 9 * tile
    return pl.pallas_call(
        functools.partial(finish_kernel, 1.0 / total_rows),
        out_shape=jax.ShapeDtypeStruct((4, n, tile), mine.dtype),
        in_specs=[vmem, vmem],
        out_specs=vmem,
        scratch_shapes=[
            pltpu.VMEM((halves, quarters, share, tile), jnp.float32),
            pltpu.VMEM((parts,) + ends.shape, ends.dtype),
            pltpu.VMEM((2, 3 * tile, 3 * tile), jnp.float32),
            pltpu.VMEM((n + tile, n + tile), jnp.float32),
            pltpu.VMEM((n + tile, n + tile), jnp.float32),
            pltpu.VMEM((n, tile), jnp.float32),
            pltpu.SemaphoreType.DMA((2, 6)),
            pltpu.SemaphoreType.DMA((2, 8)),
            pltpu.SemaphoreType.DMA((2, 7)),
            pltpu.SemaphoreType.DMA((2, 9)),
            pltpu.SemaphoreType.DMA((2, 9)),
        ],
        compiler_params=pltpu.CompilerParams(
            collective_id=1, has_side_effects=True, vmem_limit_bytes=48 * 2 ** 20),
    )(mine, ends)


def direct_body(line_columns, line_widths, layer_owner):
    total_rows = lax.axis_size("dp") * lax.axis_size("owner") * line_columns.shape[1]
    ends = jnp.cumsum(line_widths[0])
    info = jnp.concatenate([ends - line_widths[0], ends]).astype(jnp.int32)
    info = jnp.broadcast_to(info[:, None], (info.shape[0], tile))
    mine, ends = reduced_part(line_columns, info)
    results = finish(mine, ends, total_rows)
    return results.at[layer_owner].get(mode="promise_in_bounds")


def solution(mesh):
    in_specs = (P(None, ("dp", "owner"), None), P(("dp", "owner"), None), P())
    chosen = direct_body if dict(mesh.shape) == {"dp": 8, "owner": 4} else body
    return jax.shard_map(chosen, mesh=mesh, in_specs=in_specs, out_specs=P(), check_vma=False)
```
